256 devices in a mesh: dp: 8 (over y, core), seq: 32 (over z, x).
Axes of the slice: x: 4, y: 4, z: 8, core: 2. Of those that a mesh axis runs over, the one named last changes fastest.
Arguments:
- query: bfloat16 [8, 32, 128, 6144], P('dp', 'seq'), may hold values from -48 to 48
- keys: bfloat16 [8, 32, 128, 6144], P('dp', 'seq'), may hold values from -48 to 48
- values: bfloat16 [8, 32, 128, 6144], P('dp', 'seq'), may hold values from -6 to 6
- grad_out: bfloat16 [8, 32, 128, 6144], P('dp', 'seq'), may hold values from -6 to 6
- frames: int32 [8], replicated, may hold values from 8 to 32, as said below
- bias: float32 [24, 63], replicated, may hold values from -2 to 2
Outputs:
- grad_query: bfloat16 [8, 32, 128, 6144], P('dp', 'seq')
- grad_keys: bfloat16 [8, 32, 128, 6144], P('dp', 'seq')
- grad_values: bfloat16 [8, 32, 128, 6144], P('dp', 'seq')
- bias_grad: float32 [24, 63], replicated
The draws below stay inside these ranges and needn't reach their ends.
Inputs may be any that keep to these rules, and one draw needn't show every extreme that they name: Some clip has 32 frames.
All inputs are finite; a program needn't handle non-finite values.
Results may differ from the reference program's by a relative error of at most 0.023.
Values may be sent and summed in bfloat16 or wider, within the bound.
No kernel may reach another device: no remote copies, remote signals or barrier semaphores. Data moves between devices by JAX's collectives and lax.ppermute only.
A program may use at most 64 MiB of HBM per device.

```python
import jax
import jax.numpy as jnp
from jax import lax

SHEADS = 24
THEADS = 24
HDIM = 128
PATCHES = 128
FRAMES = 32
CLIPS = 8


def drawn_rows(key):
    full_shape = (CLIPS, FRAMES, PATCHES, (SHEADS + THEADS) * HDIM)
    levels = jax.random.randint(jax.random.fold_in(key, 12), (CLIPS, FRAMES, PATCHES, 1), 0, 3)
    amplitude = 4.0 + 2.0 * levels.astype(jnp.float32)
    direction = jnp.clip(jax.random.normal(jax.random.fold_in(key, 13), full_shape, jnp.float32), -6.0, 6.0)
    return amplitude * direction


def draw_query(key, part):
    strong = drawn_rows(key)
    key = jax.random.fold_in(key, 1)
    regular = jnp.clip(jax.random.normal(key, strong.shape, jnp.float32), -6.0, 6.0)
    return regular.astype(jnp.bfloat16)


def draw_keys(key, part):
    strong = drawn_rows(key)
    key = jax.random.fold_in(key, 2)
    regular = jnp.clip(jax.random.normal(key, strong.shape, jnp.float32), -6.0, 6.0)
    return regular.astype(jnp.bfloat16)


def draw_frames(key, part):
    key = jax.random.fold_in(key, 3)
    lowest = max(FRAMES // 4, 1)
    lengths = jax.random.randint(key, (CLIPS,), lowest, FRAMES + 1)
    chosen = jax.random.randint(jax.random.fold_in(key, 4), (), 0, CLIPS)
    return jnp.where(jnp.arange(CLIPS) == chosen, FRAMES, lengths).astype(jnp.int32)


def block_scale(rng, shape, pieces, smallest, top_value):
    gain = 1.0
    for axis_at, blocks in pieces:
        draws = jax.random.uniform(jax.random.fold_in(jax.random.fold_in(rng, 6), axis_at), (blocks,), jnp.float32, smallest / len(pieces), top_value / len(pieces))
        gain = gain * jnp.repeat(jnp.exp(draws), shape[axis_at] // blocks).reshape((-1,) + (1,) * (len(shape) - 1 - axis_at))
    return gain


def noise(rng, shape, scale, reach, split=(), dtype=jnp.bfloat16):
    values = jax.random.normal(rng, shape, jnp.float32) * scale
    if len(split) > 0:
        values = block_scale(rng, shape, split, -0.22, 0.18) * values
    return jnp.clip(values, min=-reach, max=reach).astype(dtype)


def setup_inputs(seed: int = 0) -> dict:
    key_of = jax.random.split(jax.random.key(seed), 7)
    query = draw_query(jax.random.fold_in(key_of[6], 71), 0)
    keys = draw_keys(jax.random.fold_in(key_of[6], 71), 0)
    values = noise(key_of[2], (CLIPS, FRAMES, PATCHES, (SHEADS + THEADS) * HDIM), 1.0, 6.0, ((0, 8), (1, 32)))
    grad_out = noise(key_of[3], (CLIPS, FRAMES, PATCHES, (SHEADS + THEADS) * HDIM), 1.0, 6.0, ((0, 8), (1, 32)))
    frames = draw_frames(jax.random.fold_in(key_of[6], 71), 0)
    bias = jnp.clip(jax.random.uniform(key_of[5], (THEADS, 2 * FRAMES - 1), jnp.float32, -2.0, 2.0), -2.0, 2.0)
    return dict(query=query, keys=keys, values=values, grad_out=grad_out, frames=frames, bias=bias)


NEG = -1e+30

def attend_grads(query, keys, values, grad_out, extra, allowed):
    wide = jnp.float32
    scale_factor = query.shape[-1] ** (-0.5)
    logits = jnp.einsum('bqhd,bkhd->bhqk', query.astype(wide), keys.astype(wide)) * scale_factor + extra
    logits = jnp.where(allowed, logits, NEG)
    row_max = lax.optimization_barrier(jnp.max(logits, axis=-1, keepdims=True))
    exponent = jnp.exp(logits - row_max)
    attention = exponent / lax.optimization_barrier(jnp.sum(exponent, axis=-1, keepdims=True))
    attention_low = attention.astype(jnp.bfloat16)
    output = jnp.einsum('bhqk,bkhd->bqhd', attention_low.astype(wide), values.astype(wide))
    row_delta = jnp.einsum('bqhd,bqhd->bhq', grad_out.astype(wide), output)
    grad_attention = jnp.einsum('bqhd,bkhd->bhqk', grad_out.astype(wide), values.astype(wide))
    grad_logits = attention * (grad_attention - row_delta[..., None])
    grad_low = grad_logits.astype(jnp.bfloat16)
    grad_query = jnp.einsum('bhqk,bkhd->bqhd', grad_low.astype(wide), keys.astype(wide)) * scale_factor
    grad_keys = jnp.einsum('bhqk,bqhd->bkhd', grad_low.astype(wide), query.astype(wide)) * scale_factor
    grad_values = jnp.einsum('bhqk,bqhd->bkhd', attention_low.astype(wide), grad_out.astype(wide))
    return (grad_query.astype(jnp.bfloat16), grad_keys.astype(jnp.bfloat16), grad_values.astype(jnp.bfloat16), grad_logits)

def offset_table(frame_count):
    positions = jnp.arange(frame_count)
    offsets = positions[None, :] - positions[:, None] + frame_count - 1
    return (offsets[:, :, None] == jnp.arange(2 * frame_count - 1)[None, None, :]).astype(jnp.float32)

def reference(query, keys, values, grad_out, frames, bias):
    onehot = offset_table(FRAMES)
    bias_table = jnp.einsum('hj,qkj->hqk', bias, onehot, precision=lax.Precision.HIGHEST)
    split_cols = SHEADS * HDIM
    frame_ids = jnp.arange(FRAMES)

    def spatial_frame(tensors):
        shaped = [tensor.reshape(1, PATCHES, SHEADS, HDIM) for tensor in tensors]
        grads = attend_grads(shaped[0], shaped[1], shaped[2], shaped[3], 0.0, True)
        return tuple((grad.reshape(PATCHES, split_cols) for grad in grads[:3]))

    def temporal_view(tensor):
        return jnp.transpose(tensor[:, :, split_cols:].reshape(FRAMES, PATCHES, THEADS, HDIM), (1, 0, 2, 3))

    def clip_work(inputs):
        clip_query, clip_keys, clip_values, clip_grad, length = inputs
        live_rows = (frame_ids < length).astype(jnp.bfloat16)
        clip_grad = clip_grad * live_rows[:, None, None]
        spatial = lax.map(spatial_frame, (clip_query[:, :, :split_cols], clip_keys[:, :, :split_cols], clip_values[:, :, :split_cols], clip_grad[:, :, :split_cols]))
        grads = attend_grads(temporal_view(clip_query), temporal_view(clip_keys), temporal_view(clip_values), temporal_view(clip_grad), bias_table[None], frame_ids < length)
        temporal = [jnp.transpose(grad, (1, 0, 2, 3)).reshape(FRAMES, PATCHES, THEADS * HDIM) for grad in grads[:3]]
        bias_part = jnp.einsum('phqk,qkj->hj', grads[3], onehot, precision=lax.Precision.HIGHEST)
        joined = tuple((jnp.concatenate([spatial[number], temporal[number]], axis=2) for number in range(3)))
        return joined + (bias_part,)
    grad_query, grad_keys, grad_values, parts = lax.map(clip_work, (query, keys, values, grad_out, frames))
    bias_grad = lax.optimization_barrier(jnp.sum(parts, axis=0)) / jnp.sqrt(jnp.float32(CLIPS * FRAMES * PATCHES))
    return (grad_query, grad_keys, grad_values, bias_grad)
```

```python
import functools

import jax
import jax.numpy as jnp
from jax import lax
from jax.experimental import pallas as pl
from jax.experimental.pallas import tpu as pltpu
from jax.sharding import PartitionSpec as P

SHEADS = 24
THEADS = 24
HDIM = 128
ROWS = 8
HALVES = 2
HEADS_HERE = THEADS // HALVES
WIDTH = HEADS_HERE * HDIM
SPATIAL = SHEADS * HDIM
SPAN = 512
NEG = -1e30
WIDE = jnp.float32
LOW = jnp.bfloat16
SCALE = HDIM ** (-0.5)
MIB = 1024 * 1024

NT = (((1,), (1,)), ((), ()))
NN = (((1,), (0,)), ((), ()))
TN = (((0,), (0,)), ((), ()))


def dot(left, right, dims):
    return lax.dot_general(left, right, dims, preferred_element_type=WIDE)


def head_grads(query, keys, values, grad, extra):
    logits = dot(keys, query, NT) * SCALE
    if extra is not None:
        logits = logits + extra
    exponent = jnp.exp(logits - jnp.max(logits, axis=0, keepdims=True))
    attention = exponent * (1.0 / jnp.sum(exponent, axis=0, keepdims=True))
    grad_attention = dot(values, grad, NT)
    row_delta = jnp.sum(attention * grad_attention, axis=0, keepdims=True)
    grad_logits = attention * (grad_attention - row_delta)
    grad_low = grad_logits.astype(LOW)
    grad_query = (dot(grad_low, keys, TN) * SCALE).astype(LOW)
    grad_keys = (dot(grad_low, query, NN) * SCALE).astype(LOW)
    grad_values = dot(attention.astype(LOW), grad, NN).astype(LOW)
    return grad_query, grad_keys, grad_values, grad_logits


def pack_kernel(query, keys, values, grad, packed, sems):
    copies = []
    for number, source in enumerate((query, keys, values, grad)):
        for half in range(HALVES):
            copies.append(
                pltpu.make_async_copy(
                    source.at[:, :, pl.ds(SPATIAL + half * WIDTH, WIDTH)],
                    packed.at[:, half, number],
                    sems.at[number * HALVES + half],
                )
            )
    for copy in copies:
        copy.start()
    for copy in copies:
        copy.wait()


def unpack_kernel(back, query_in, keys_in, values_in, query, keys, values, sems):
    copies = []
    for number, target in enumerate((query, keys, values)):
        for half in range(HALVES):
            copies.append(
                pltpu.make_async_copy(
                    back.at[:, half, number],
                    target.at[:, :, pl.ds(SPATIAL + half * WIDTH, WIDTH)],
                    sems.at[number * HALVES + half],
                )
            )
    for copy in copies:
        copy.start()
    for copy in copies:
        copy.wait()


def spatial_kernel(heads, live, query, keys, values, grad, grad_query, grad_keys, grad_values):
    flag = live[0].astype(WIDE).astype(LOW)
    for head in range(heads):
        cols = pl.ds(head * HDIM, HDIM)
        outs = head_grads(
            query[:, cols], keys[:, cols], values[:, cols], grad[:, cols] * flag, None
        )
        grad_query[:, cols] = outs[0]
        grad_keys[:, cols] = outs[1]
        grad_values[:, cols] = outs[2]


def table_kernel(frame_count, length, seed, table):
    shape = (ROWS, frame_count * ROWS)
    for frame in range(frame_count):
        row = seed[0]
        moved = pltpu.roll(row, frame * ROWS, 1) if frame else row
        allowed = jnp.full(shape, frame, jnp.int32) < length[0]
        table[0, pl.ds(frame * ROWS, ROWS), :] = jnp.where(allowed, moved[:, : shape[1]], NEG)


def temporal_kernel(frame_count, length, tensors, table, grads, bias_part):
    tokens = frame_count * ROWS
    live_rows = lax.broadcasted_iota(jnp.int32, (tokens, HDIM), 0) < length[0] * ROWS

    def one_head(head):
        cols = pl.ds(pl.multiple_of(head * HDIM, HDIM), HDIM)
        query, keys, values, grad = (
            tensors[:, number, :, cols].reshape(tokens, HDIM) for number in range(4)
        )
        grad = jnp.where(live_rows, grad.astype(WIDE), 0.0).astype(LOW)
        outs = head_grads(query, keys, values, grad, table[head])
        for number in range(3):
            grads[:, number, :, cols] = outs[number].reshape(frame_count, ROWS, HDIM)
        terms = outs[3].reshape(frame_count, ROWS, tokens)
        parts = [
            jnp.concatenate([terms[frame], jnp.zeros((ROWS, SPAN - tokens), WIDE)], axis=1)
            for frame in range(frame_count)
        ]
        step = ROWS
        while len(parts) > 1:
            parts = [
                parts[at] + pltpu.roll(parts[at + 1], SPAN - step, 1)
                for at in range(0, len(parts), 2)
            ]
            step *= 2
        bias_part[head] = parts[0]

    def pair(at, carry):
        one_head(2 * at)
        one_head(2 * at + 1)
        return carry

    lax.fori_loop(0, HEADS_HERE // 2, pair, 0)


def spec(space):
    return pl.BlockSpec(memory_space=space)


def params(limit):
    return pltpu.CompilerParams(vmem_limit_bytes=limit * MIB)


def butterfly(value, axis):
    count = lax.axis_size(axis)
    step = 1
    while step < count:
        value = value + lax.ppermute(value, axis, [(at, at ^ step) for at in range(count)])
        step *= 2
    return value


def local(query, keys, values, grad_out, frames, bias):
    frame_count = lax.axis_size("seq")
    frame_index = lax.axis_index("seq")
    length = lax.dynamic_index_in_dim(frames, lax.axis_index("dp"), 0, keepdims=True)
    live = (frame_index < length).astype(jnp.int32)
    patches, columns = query.shape[2], query.shape[3]
    groups = patches // ROWS
    tokens = frame_count * ROWS
    flat = [tensor.reshape(patches, columns) for tensor in (query, keys, values, grad_out)]
    tiled = [tensor.reshape(groups, ROWS, columns) for tensor in flat]

    packed = pl.pallas_call(
        pack_kernel,
        out_shape=jax.ShapeDtypeStruct((groups, HALVES, 4, ROWS, WIDTH), LOW),
        in_specs=[spec(pltpu.HBM)] * 4,
        out_specs=spec(pltpu.VMEM),
        scratch_shapes=[pltpu.SemaphoreType.DMA((4 * HALVES,))],
        compiler_params=params(60),
        name="pack",
    )(*tiled)
    gathered = lax.all_to_all(
        packed.reshape(frame_count, 4, ROWS, WIDTH), "seq", split_axis=0, concat_axis=0, tiled=True
    )

    heads = 4
    block = pl.BlockSpec((patches, heads * HDIM), lambda at, live: (0, at))
    spatial = pl.pallas_call(
        functools.partial(spatial_kernel, heads),
        out_shape=[jax.ShapeDtypeStruct((patches, columns), LOW)] * 3,
        grid_spec=pltpu.PrefetchScalarGridSpec(
            num_scalar_prefetch=1,
            grid=(SHEADS // heads,),
            in_specs=[block] * 4,
            out_specs=[block] * 3,
        ),
        compiler_params=params(48),
        cost_estimate=pl.CostEstimate(
            flops=10 * SHEADS * patches * patches * HDIM,
            bytes_accessed=14 * patches * SPATIAL,
            transcendentals=SHEADS * patches * patches,
        ),
        name="spatial",
    )(live, *flat)

    half = frame_index % HALVES
    bias_here = lax.dynamic_slice_in_dim(bias, half * HEADS_HERE, HEADS_HERE, 0)
    offsets = jnp.concatenate(
        [
            bias_here[:, :frame_count][:, ::-1],
            jnp.full((HEADS_HERE, 1), NEG, WIDE),
            bias_here[:, frame_count:][:, ::-1],
        ],
        axis=1,
    )
    seed = jnp.where(
        jnp.eye(ROWS, dtype=bool)[None, :, None, :], offsets[:, None, :, None], NEG
    ).reshape(HEADS_HERE, ROWS, SPAN)
    table = pl.pallas_call(
        functools.partial(table_kernel, frame_count),
        out_shape=jax.ShapeDtypeStruct((HEADS_HERE, tokens, tokens), WIDE),
        grid_spec=pltpu.PrefetchScalarGridSpec(
            num_scalar_prefetch=1,
            grid=(HEADS_HERE,),
            in_specs=[pl.BlockSpec((1, ROWS, SPAN), lambda at, length: (at, 0, 0))],
            out_specs=pl.BlockSpec((1, tokens, tokens), lambda at, length: (at, 0, 0)),
        ),
        compiler_params=params(48),
        cost_estimate=pl.CostEstimate(
            flops=HEADS_HERE * tokens * tokens * 4,
            bytes_accessed=HEADS_HERE * tokens * tokens * 4,
            transcendentals=0,
        ),
        name="table",
    )(length, seed)

    gathered, table, *spatial = lax.optimization_barrier((gathered, table, *spatial))
    grads, bias_part = pl.pallas_call(
        functools.partial(temporal_kernel, frame_count),
        out_shape=[
            jax.ShapeDtypeStruct((frame_count, 3, ROWS, WIDTH), LOW),
            jax.ShapeDtypeStruct((HEADS_HERE, ROWS, SPAN), WIDE),
        ],
        in_specs=[spec(pltpu.SMEM), spec(pltpu.VMEM), spec(pltpu.VMEM)],
        out_specs=[spec(pltpu.VMEM), spec(pltpu.VMEM)],
        compiler_params=params(48),
        cost_estimate=pl.CostEstimate(
            flops=10 * HEADS_HERE * tokens * tokens * HDIM,
            bytes_accessed=14 * tokens * WIDTH + 4 * HEADS_HERE * tokens * tokens,
            transcendentals=HEADS_HERE * tokens * tokens,
        ),
        name="temporal",
    )(length, gathered, table)

    back = lax.all_to_all(grads, "seq", split_axis=0, concat_axis=0, tiled=True)

    offset_sums = jnp.sum(
        bias_part.reshape(HEADS_HERE, ROWS, SPAN // ROWS, ROWS), axis=(1, 3)
    )
    sums = lax.dynamic_update_slice_in_dim(
        jnp.zeros((THEADS, SPAN // ROWS), WIDE), offset_sums, half * HEADS_HERE, 0
    )
    total = butterfly(butterfly(sums, "dp"), "seq")
    ordered = jnp.concatenate(
        [total[:, :frame_count][:, ::-1], total[:, frame_count + 1 :][:, ::-1]], axis=1
    )
    bias_grad = ordered / jnp.sqrt(WIDE(lax.axis_size("dp") * frame_count * patches))

    outputs = pl.pallas_call(
        unpack_kernel,
        out_shape=[jax.ShapeDtypeStruct((groups, ROWS, columns), LOW)] * 3,
        in_specs=[spec(pl.ANY)] + [spec(pltpu.HBM)] * 3,
        out_specs=[spec(pltpu.HBM)] * 3,
        scratch_shapes=[pltpu.SemaphoreType.DMA((3 * HALVES,))],
        input_output_aliases={1: 0, 2: 1, 3: 2},
        compiler_params=params(48),
        name="unpack",
    )(
        back.reshape(groups, HALVES, 3, ROWS, WIDTH),
        *(tensor.reshape(groups, ROWS, columns) for tensor in spatial),
    )
    shaped = tuple(tensor.reshape(1, 1, patches, columns) for tensor in outputs)
    return (*shaped, bias_grad)


def solution(mesh):
    split = P("dp", "seq", None, None)
    return jax.shard_map(
        local,
        mesh=mesh,
        in_specs=(split, split, split, split, P(), P()),
        out_specs=(split, split, split, P()),
        check_vma=False,
    )
```

```python
import functools

import jax
import jax.numpy as jnp
from jax import lax
from jax.experimental import pallas as pl
from jax.experimental.pallas import tpu as pltpu
from jax.sharding import PartitionSpec as P

SHEADS = 24
THEADS = 24
HDIM = 128
ROWS = 8
HALVES = 2
HEADS_HERE = THEADS // HALVES
WIDTH = HEADS_HERE * HDIM
SPATIAL = SHEADS * HDIM
SPAN = 512
NEG = -1e30
LOG2E = 1.4426950408889634
WIDE = jnp.float32
LOW = jnp.bfloat16
SCALE = HDIM ** (-0.5)
MIB = 1024 * 1024

NT = (((1,), (1,)), ((), ()))
NN = (((1,), (0,)), ((), ()))
TN = (((0,), (0,)), ((), ()))


def dot(left, right, dims):
    return lax.dot_general(left, right, dims, preferred_element_type=WIDE)


def head_grads(query, keys, values, grad, extra):
    logits = dot(keys, query, NT) * (SCALE * LOG2E)
    if extra is not None:
        logits = logits + extra
    exponent = jnp.exp2(logits - jnp.max(logits, axis=0, keepdims=True))
    attention = exponent * (1.0 / jnp.sum(exponent, axis=0, keepdims=True))
    grad_attention = dot(values, grad, NT)
    row_delta = jnp.sum(attention * grad_attention, axis=0, keepdims=True)
    grad_logits = attention * (grad_attention - row_delta)
    grad_low = grad_logits.astype(LOW)
    grad_query = (dot(grad_low, keys, TN) * SCALE).astype(LOW)
    grad_keys = (dot(grad_low, query, NN) * SCALE).astype(LOW)
    grad_values = dot(attention.astype(LOW), grad, NN).astype(LOW)
    return grad_query, grad_keys, grad_values, grad_logits


def pack_kernel(query, keys, values, grad, packed, staged, in_sems, out_sems):
    reads, writes = [], []
    for number, source in enumerate((query, keys, values, grad)):
        for half in range(HALVES):
            at = number * HALVES + half
            reads.append(
                pltpu.make_async_copy(
                    source.at[:, :, pl.ds(SPATIAL + half * WIDTH, WIDTH)],
                    staged.at[:, half, number],
                    in_sems.at[at],
                )
            )
            writes.append(
                pltpu.make_async_copy(
                    staged.at[:, half, number], packed.at[:, half, number], out_sems.at[at]
                )
            )
    for copy in reads:
        copy.start()
    for read, write in zip(reads, writes):
        read.wait()
        write.start()
    for copy in writes:
        copy.wait()


def unpack_kernel(back, query_in, keys_in, values_in, query, keys, values, sems):
    copies = []
    for number, target in enumerate((query, keys, values)):
        for half in range(HALVES):
            copies.append(
                pltpu.make_async_copy(
                    back.at[:, half, number],
                    target.at[:, :, pl.ds(SPATIAL + half * WIDTH, WIDTH)],
                    sems.at[number * HALVES + half],
                )
            )
    for copy in copies:
        copy.start()
    for copy in copies:
        copy.wait()


def spatial_kernel(heads, live, query, keys, values, grad, grad_query, grad_keys, grad_values):
    flag = live[0].astype(WIDE).astype(LOW)
    for head in range(heads):
        cols = pl.ds(head * HDIM, HDIM)
        outs = head_grads(
            query[:, cols], keys[:, cols], values[:, cols], grad[:, cols] * flag, None
        )
        grad_query[:, cols] = outs[0]
        grad_keys[:, cols] = outs[1]
        grad_values[:, cols] = outs[2]


def moved_rows(seed, frame_count, length):
    blocks = SPAN // HDIM
    turns = HDIM // ROWS
    wide = frame_count * ROWS // HDIM
    rows = [None] * frame_count
    for turn in range(turns):
        moved = pltpu.roll(seed, turn * ROWS, 1) if turn else seed
        pieces = [moved[:, at * HDIM : (at + 1) * HDIM] for at in range(blocks)]
        for frame in range(turn, frame_count, turns):
            shift = frame // turns
            joined = jnp.concatenate([pieces[(at - shift) % blocks] for at in range(wide)], axis=1)
            rows[frame] = jnp.where(frame < length, joined, NEG)
    return jnp.concatenate(rows, axis=0)


def offset_sums(terms, frame_count):
    blocks = SPAN // HDIM
    turns = HDIM // ROWS
    wide = frame_count * ROWS // HDIM
    parts = []
    for turn in range(turns):
        pieces = [None] * blocks
        for frame in range(turn, frame_count, turns):
            for at in range(wide):
                to = (at - frame // turns) % blocks
                piece = terms[frame][:, at * HDIM : (at + 1) * HDIM]
                pieces[to] = piece if pieces[to] is None else pieces[to] + piece
        pieces = [jnp.zeros((ROWS, HDIM), WIDE) if piece is None else piece for piece in pieces]
        parts.append(jnp.concatenate(pieces, axis=1))
    step = ROWS
    while len(parts) > 1:
        parts = [
            parts[at] + pltpu.roll(parts[at + 1], SPAN - step, 1)
            for at in range(0, len(parts), 2)
        ]
        step *= 2
    return parts[0]


def temporal_kernel(
    frame_count, heads, length, tensors, seed, grads, bias_part, staged, sems
):
    tokens = frame_count * ROWS
    live_rows = lax.broadcasted_iota(jnp.int32, (tokens, HDIM), 0) < length[0] * ROWS

    def one_head(head):
        cols = pl.ds(pl.multiple_of(head * HDIM, HDIM), HDIM)
        query, keys, values, grad = (
            tensors[:, number, :, cols].reshape(tokens, HDIM) for number in range(4)
        )
        grad = jnp.where(live_rows, grad.astype(WIDE), 0.0).astype(LOW)
        table = moved_rows(seed[head], frame_count, length[0])
        outs = head_grads(query, keys, values, grad, table)
        for number in range(3):
            staged[:, number, :, cols] = outs[number].reshape(frame_count, ROWS, HDIM)
        terms = outs[3].reshape(frame_count, ROWS, tokens)
        bias_part[head] = offset_sums(terms, frame_count)

    def write(at):
        cols = pl.ds(pl.multiple_of(at * heads * HDIM, HDIM), heads * HDIM)
        return pltpu.make_async_copy(
            staged.at[:, :, :, cols], grads.at[:, :, :, cols], sems.at[at]
        )

    def step(at, carry):
        for offset in range(heads):
            one_head(at * heads + offset)
        write(at).start()
        return carry

    def finish(at, carry):
        write(at).wait()
        return carry

    lax.fori_loop(0, HEADS_HERE // heads, step, 0)
    lax.fori_loop(0, HEADS_HERE // heads, finish, 0)


def spec(space):
    return pl.BlockSpec(memory_space=space)


def place(space, *arrays):
    return [pltpu.with_memory_space_constraint(array, space) for array in arrays]


def params(limit):
    return pltpu.CompilerParams(vmem_limit_bytes=limit * MIB)


def exchange_sum(value, axis, steps):
    count = lax.axis_size(axis)
    pieces = [value] + [
        lax.ppermute(value, axis, [(at, at ^ step) for at in range(count)]) for step in steps
    ]
    while len(pieces) > 1:
        pieces = [pieces[at] + pieces[at + 1] for at in range(0, len(pieces), 2)]
    return pieces[0]


def local(query, keys, values, grad_out, frames, bias):
    frame_count = lax.axis_size("seq")
    frame_index = lax.axis_index("seq")
    length = lax.dynamic_index_in_dim(frames, lax.axis_index("dp"), 0, keepdims=True)
    live = (frame_index < length).astype(jnp.int32)
    patches, columns = query.shape[2], query.shape[3]
    groups = patches // ROWS
    tokens = frame_count * ROWS
    flat = [tensor.reshape(patches, columns) for tensor in (query, keys, values, grad_out)]
    tiled = [tensor.reshape(groups, ROWS, columns) for tensor in flat]

    packed = pl.pallas_call(
        pack_kernel,
        out_shape=pltpu.HBM((groups, HALVES, 4, ROWS, WIDTH), LOW),
        in_specs=[spec(pl.ANY)] * 4,
        out_specs=spec(pl.ANY),
        scratch_shapes=[
            pltpu.VMEM((groups, HALVES, 4, ROWS, WIDTH), LOW),
            pltpu.SemaphoreType.DMA((4 * HALVES,)),
            pltpu.SemaphoreType.DMA((4 * HALVES,)),
        ],
        compiler_params=params(8),
        name="pack",
    )(*place(pltpu.HBM, *tiled))
    gathered = lax.all_to_all(
        packed.reshape(frame_count, 4, ROWS, WIDTH), "seq", split_axis=0, concat_axis=0, tiled=True
    )

    heads = 4
    block = pl.BlockSpec((patches, heads * HDIM), lambda at, live: (0, at))
    spatial = pl.pallas_call(
        functools.partial(spatial_kernel, heads),
        out_shape=[pltpu.HBM((patches, columns), LOW)] * 3,
        grid_spec=pltpu.PrefetchScalarGridSpec(
            num_scalar_prefetch=1,
            grid=(SHEADS // heads,),
            in_specs=[block] * 4,
            out_specs=[block] * 3,
        ),
        compiler_params=params(16),
        cost_estimate=pl.CostEstimate(
            flops=10 * SHEADS * patches * patches * HDIM,
            bytes_accessed=14 * patches * SPATIAL,
            transcendentals=SHEADS * patches * patches,
        ),
        name="spatial",
    )(live, *place(pltpu.HBM, *flat))

    half = frame_index % HALVES
    bias_here = lax.dynamic_slice_in_dim(bias, half * HEADS_HERE, HEADS_HERE, 0)
    bias_here = bias_here * LOG2E
    offsets = jnp.concatenate(
        [
            bias_here[:, :frame_count][:, ::-1],
            jnp.full((HEADS_HERE, 1), NEG, WIDE),
            bias_here[:, frame_count:][:, ::-1],
        ],
        axis=1,
    )
    seed = jnp.where(
        jnp.eye(ROWS, dtype=bool)[None, :, None, :], offsets[:, None, :, None], NEG
    ).reshape(HEADS_HERE, ROWS, SPAN)
    gathered, *spatial = lax.optimization_barrier((gathered, *spatial))
    grads, bias_part = pl.pallas_call(
        functools.partial(temporal_kernel, frame_count, heads),
        out_shape=[
            pltpu.HBM((frame_count, 3, ROWS, WIDTH), LOW),
            pltpu.VMEM((HEADS_HERE, ROWS, SPAN), WIDE),
        ],
        in_specs=[spec(pltpu.SMEM), spec(pltpu.VMEM), spec(pltpu.VMEM)],
        out_specs=[spec(pl.ANY), spec(pltpu.VMEM)],
        scratch_shapes=[
            pltpu.VMEM((frame_count, 3, ROWS, WIDTH), LOW),
            pltpu.SemaphoreType.DMA((HEADS_HERE // heads,)),
        ],
        compiler_params=params(16),
        cost_estimate=pl.CostEstimate(
            flops=10 * HEADS_HERE * tokens * tokens * HDIM,
            bytes_accessed=14 * tokens * WIDTH,
            transcendentals=HEADS_HERE * tokens * tokens,
        ),
        name="temporal",
    )(length, *place(pltpu.VMEM, gathered, seed))

    back = lax.all_to_all(grads, "seq", split_axis=0, concat_axis=0, tiled=True)

    sums = jnp.sum(bias_part.reshape(HEADS_HERE, ROWS, SPAN // ROWS, ROWS), axis=(1, 3))
    sums = jnp.concatenate(
        [sums[:, :frame_count][:, ::-1], sums[:, frame_count + 1 :][:, ::-1]], axis=1
    ) / jnp.sqrt(WIDE(lax.axis_size("dp") * frame_count * patches))
    sums = lax.dynamic_update_slice_in_dim(
        jnp.zeros((THEADS, 2 * frame_count - 1), WIDE), sums, half * HEADS_HERE, 0
    )
    for axis, steps in (("dp", (1,)), ("dp", (2, 4, 6)), ("seq", (1, 2, 3)), ("seq", (4, 8, 12))):
        sums = exchange_sum(sums, axis, steps)
    back, sums = lax.optimization_barrier((back, sums))
    bias_grad = exchange_sum(sums, "seq", (16,))

    outputs = pl.pallas_call(
        unpack_kernel,
        out_shape=[pltpu.HBM((groups, ROWS, columns), LOW)] * 3,
        in_specs=[spec(pl.ANY)] * 4,
        out_specs=[spec(pl.ANY)] * 3,
        scratch_shapes=[pltpu.SemaphoreType.DMA((3 * HALVES,))],
        input_output_aliases={1: 0, 2: 1, 3: 2},
        compiler_params=params(8),
        cost_estimate=pl.CostEstimate(
            flops=0, bytes_accessed=12 * patches * SPATIAL, transcendentals=0
        ),
        name="unpack",
    )(
        back.reshape(groups, HALVES, 3, ROWS, WIDTH),
        *place(pltpu.HBM, *(tensor.reshape(groups, ROWS, columns) for tensor in spatial)),
    )
    shaped = tuple(tensor.reshape(1, 1, patches, columns) for tensor in outputs)
    return (*shaped, bias_grad)


def solution(mesh):
    split = P("dp", "seq", None, None)
    return jax.shard_map(
        local,
        mesh=mesh,
        in_specs=(split, split, split, split, P(), P()),
        out_specs=(split, split, split, P()),
        check_vma=False,
    )
```

```python
import functools

import jax
import jax.numpy as jnp
from jax import lax
from jax.experimental import pallas as pl
from jax.experimental.pallas import tpu as pltpu
from jax.sharding import PartitionSpec as P

SHEADS = 24
THEADS = 24
HDIM = 128
ROWS = 8
HALVES = 2
HEADS_HERE = THEADS // HALVES
WIDTH = HEADS_HERE * HDIM
SPATIAL = SHEADS * HDIM
SPAN = 512
NEG = -1e30
LOG2E = 1.4426950408889634
WIDE = jnp.float32
LOW = jnp.bfloat16
SCALE = HDIM ** (-0.5)
MIB = 1024 * 1024

NT = (((1,), (1,)), ((), ()))
NN = (((1,), (0,)), ((), ()))
TN = (((0,), (0,)), ((), ()))


def dot(left, right, dims):
    return lax.dot_general(left, right, dims, preferred_element_type=WIDE)


def products(query, keys, values, grad):
    return dot(keys, query, NT), dot(values, grad, NT)


def soften(logits, grad_attention, extra):
    logits = logits * (SCALE * LOG2E)
    if extra is not None:
        logits = logits + extra
    exponent = jnp.exp2(logits - jnp.max(logits, axis=0, keepdims=True))
    attention = exponent * (1.0 / jnp.sum(exponent, axis=0, keepdims=True))
    row_delta = jnp.sum(attention * grad_attention, axis=0, keepdims=True)
    return attention.astype(LOW), attention * (grad_attention - row_delta)


def token_grads(attention_low, grad_low, query, keys, grad):
    grad_query = (dot(grad_low, keys, TN) * SCALE).astype(LOW)
    grad_keys = (dot(grad_low, query, NN) * SCALE).astype(LOW)
    grad_values = dot(attention_low, grad, NN).astype(LOW)
    return grad_query, grad_keys, grad_values


def pack_kernel(query, keys, values, grad, packed, staged, in_sems, out_sems):
    reads, writes = [], []
    for number, source in enumerate((query, keys, values, grad)):
        for half in range(HALVES):
            at = number * HALVES + half
            reads.append(
                pltpu.make_async_copy(
                    source.at[:, :, pl.ds(SPATIAL + half * WIDTH, WIDTH)],
                    staged.at[:, half, number],
                    in_sems.at[at],
                )
            )
            writes.append(
                pltpu.make_async_copy(
                    staged.at[:, half, number], packed.at[:, half, number], out_sems.at[at]
                )
            )
    for copy in reads:
        copy.start()
    for read, write in zip(reads, writes):
        read.wait()
        write.start()
    for copy in writes:
        copy.wait()


def unpack_kernel(back, query_in, keys_in, values_in, query, keys, values, sems):
    copies = []
    for number, target in enumerate((query, keys, values)):
        for half in range(HALVES):
            copies.append(
                pltpu.make_async_copy(
                    back.at[:, half, number],
                    target.at[:, :, pl.ds(SPATIAL + half * WIDTH, WIDTH)],
                    sems.at[number * HALVES + half],
                )
            )
    for copy in copies:
        copy.start()
    for copy in copies:
        copy.wait()


def spatial_kernel(heads, live, query, keys, values, grad, grad_query, grad_keys, grad_values):
    flag = live[0].astype(WIDE).astype(LOW)
    for head in range(heads):
        cols = pl.ds(head * HDIM, HDIM)
        tokens = query[:, cols], keys[:, cols], values[:, cols], grad[:, cols] * flag
        attention_low, grad_logits = soften(*products(*tokens), None)
        outs = token_grads(
            attention_low, grad_logits.astype(LOW), tokens[0], tokens[1], tokens[3]
        )
        grad_query[:, cols] = outs[0]
        grad_keys[:, cols] = outs[1]
        grad_values[:, cols] = outs[2]


def moved_rows(seed, frame_count, length):
    blocks = SPAN // HDIM
    turns = HDIM // ROWS
    wide = frame_count * ROWS // HDIM
    rows = [None] * frame_count
    for turn in range(turns):
        moved = pltpu.roll(seed, turn * ROWS, 1) if turn else seed
        pieces = [moved[:, at * HDIM : (at + 1) * HDIM] for at in range(blocks)]
        for frame in range(turn, frame_count, turns):
            shift = frame // turns
            joined = jnp.concatenate([pieces[(at - shift) % blocks] for at in range(wide)], axis=1)
            rows[frame] = jnp.where(frame < length, joined, NEG)
    return jnp.concatenate(rows, axis=0)


def offset_sums(terms, frame_count):
    blocks = SPAN // HDIM
    turns = HDIM // ROWS
    wide = frame_count * ROWS // HDIM
    parts = []
    for turn in range(turns):
        pieces = [None] * blocks
        for frame in range(turn, frame_count, turns):
            for at in range(wide):
                to = (at - frame // turns) % blocks
                piece = terms[frame][:, at * HDIM : (at + 1) * HDIM]
                pieces[to] = piece if pieces[to] is None else pieces[to] + piece
        pieces = [jnp.zeros((ROWS, HDIM), WIDE) if piece is None else piece for piece in pieces]
        parts.append(jnp.concatenate(pieces, axis=1))
    step = ROWS
    while len(parts) > 1:
        parts = [
            parts[at] + pltpu.roll(parts[at + 1], SPAN - step, 1)
            for at in range(0, len(parts), 2)
        ]
        step *= 2
    return parts[0]


def temporal_kernel(frame_count, length, tensors, seed, grads, grad_logits, staged, kept, sems):
    tokens = frame_count * ROWS
    live_rows = lax.broadcasted_iota(jnp.int32, (tokens, HDIM), 0) < length[0] * ROWS
    copies = []

    def load(head):
        cols = pl.ds(head * HDIM, HDIM)
        query, keys, values, grad = (
            tensors[:, number, :, cols].reshape(tokens, HDIM) for number in range(4)
        )
        return query, keys, values, jnp.where(live_rows, grad.astype(WIDE), 0.0).astype(LOW)

    def send(source, target, at):
        copy = pltpu.make_async_copy(source, target, sems.at[at])
        copy.start()
        copies.append(copy)

    def finish(head, held, attention_low, grad_low):
        outs = token_grads(attention_low, grad_low, held[0], held[1], held[3])
        for number in range(3):
            staged[:, number, :, pl.ds(head * HDIM, HDIM)] = outs[number].reshape(
                frame_count, ROWS, HDIM
            )
        if head % 2:
            cols = pl.ds((head - 1) * HDIM, 2 * HDIM)
            send(staged.at[:, :, :, cols], grads.at[:, :, :, cols], HEADS_HERE + head // 2)

    held = load(0)
    ready = products(*held)
    waiting = None
    for head in range(HEADS_HERE):
        held_next = ready_next = None
        if head + 1 < HEADS_HERE:
            held_next = load(head + 1)
            ready_next = products(*held_next)
        table = moved_rows(seed[head], frame_count, length[0])
        attention_low, logits_grad = soften(*ready, table)
        kept[head] = logits_grad
        send(kept.at[head], grad_logits.at[head], head)
        if waiting is not None:
            finish(*waiting)
        waiting = head, held, attention_low, logits_grad.astype(LOW)
        held, ready = held_next, ready_next
    finish(*waiting)
    for copy in copies:
        copy.wait()


def bias_kernel(frame_count, terms, sums):
    sums[0] = offset_sums(terms[0].reshape(frame_count, ROWS, -1), frame_count)


def spec(space):
    return pl.BlockSpec(memory_space=space)


def place(space, *arrays):
    return [pltpu.with_memory_space_constraint(array, space) for array in arrays]


def params(limit):
    return pltpu.CompilerParams(vmem_limit_bytes=limit * MIB)


def tree_sum(pieces):
    while len(pieces) > 1:
        pieces = [pieces[at] + pieces[at + 1] for at in range(0, len(pieces), 2)]
    return pieces[0]


def exchange_sum(value, axis, steps):
    count = lax.axis_size(axis)
    return tree_sum(
        [value]
        + [lax.ppermute(value, axis, [(at, at ^ step) for at in range(count)]) for step in steps]
    )


def split_sum(value, low_steps, high_steps):
    clips, count = lax.axis_size("dp"), lax.axis_size("seq")
    pieces = []
    for steps in zip(low_steps, high_steps):
        pairs = [
            (clip * count + at, clip * count + (at ^ steps[clip % 2]))
            for clip in range(clips)
            for at in range(count)
        ]
        pieces.append(lax.ppermute(value, ("dp", "seq"), pairs))
    return tree_sum(pieces)


def local(query, keys, values, grad_out, frames, bias):
    frame_count = lax.axis_size("seq")
    frame_index = lax.axis_index("seq")
    length = lax.dynamic_index_in_dim(frames, lax.axis_index("dp"), 0, keepdims=True)
    live = (frame_index < length).astype(jnp.int32)
    patches, columns = query.shape[2], query.shape[3]
    groups = patches // ROWS
    tokens = frame_count * ROWS
    flat = [tensor.reshape(patches, columns) for tensor in (query, keys, values, grad_out)]
    tiled = [tensor.reshape(groups, ROWS, columns) for tensor in flat]

    packed = pl.pallas_call(
        pack_kernel,
        out_shape=pltpu.HBM((groups, HALVES, 4, ROWS, WIDTH), LOW),
        in_specs=[spec(pl.ANY)] * 4,
        out_specs=spec(pl.ANY),
        scratch_shapes=[
            pltpu.VMEM((groups, HALVES, 4, ROWS, WIDTH), LOW),
            pltpu.SemaphoreType.DMA((4 * HALVES,)),
            pltpu.SemaphoreType.DMA((4 * HALVES,)),
        ],
        compiler_params=params(8),
        name="pack",
    )(*place(pltpu.HBM, *tiled))
    gathered = lax.all_to_all(
        packed.reshape(frame_count, 4, ROWS, WIDTH), "seq", split_axis=0, concat_axis=0, tiled=True
    )

    heads = 4
    block = pl.BlockSpec((patches, heads * HDIM), lambda at, live: (0, at))
    spatial = pl.pallas_call(
        functools.partial(spatial_kernel, heads),
        out_shape=[pltpu.HBM((patches, columns), LOW)] * 3,
        grid_spec=pltpu.PrefetchScalarGridSpec(
            num_scalar_prefetch=1,
            grid=(SHEADS // heads,),
            in_specs=[block] * 4,
            out_specs=[block] * 3,
        ),
        compiler_params=params(16),
        cost_estimate=pl.CostEstimate(
            flops=10 * SHEADS * patches * patches * HDIM,
            bytes_accessed=14 * patches * SPATIAL,
            transcendentals=SHEADS * patches * patches,
        ),
        name="spatial",
    )(live, *place(pltpu.HBM, *flat))

    half = frame_index % HALVES
    bias_here = lax.dynamic_slice_in_dim(bias, half * HEADS_HERE, HEADS_HERE, 0)
    bias_here = bias_here * LOG2E
    offsets = jnp.concatenate(
        [
            bias_here[:, :frame_count][:, ::-1],
            jnp.full((HEADS_HERE, 1), NEG, WIDE),
            bias_here[:, frame_count:][:, ::-1],
        ],
        axis=1,
    )
    seed = jnp.where(
        jnp.eye(ROWS, dtype=bool)[None, :, None, :], offsets[:, None, :, None], NEG
    ).reshape(HEADS_HERE, ROWS, SPAN)
    gathered, *spatial = lax.optimization_barrier((gathered, *spatial))
    grads, grad_logits = pl.pallas_call(
        functools.partial(temporal_kernel, frame_count),
        out_shape=[
            pltpu.HBM((frame_count, 3, ROWS, WIDTH), LOW),
            pltpu.HBM((HEADS_HERE, tokens, tokens), WIDE),
        ],
        in_specs=[spec(pltpu.SMEM), spec(pltpu.VMEM), spec(pltpu.VMEM)],
        out_specs=[spec(pl.ANY)] * 2,
        scratch_shapes=[
            pltpu.VMEM((frame_count, 3, ROWS, WIDTH), LOW),
            pltpu.VMEM((HEADS_HERE, tokens, tokens), WIDE),
            pltpu.SemaphoreType.DMA((HEADS_HERE + HEADS_HERE // 2,)),
        ],
        compiler_params=params(24),
        cost_estimate=pl.CostEstimate(
            flops=10 * HEADS_HERE * tokens * tokens * HDIM,
            bytes_accessed=14 * tokens * WIDTH,
            transcendentals=HEADS_HERE * tokens * tokens,
        ),
        name="temporal",
    )(length, *place(pltpu.VMEM, gathered, seed))
    bias_part = pl.pallas_call(
        functools.partial(bias_kernel, frame_count),
        out_shape=jax.ShapeDtypeStruct((HEADS_HERE, ROWS, SPAN), WIDE),
        grid=(HEADS_HERE,),
        in_specs=[pl.BlockSpec((1, tokens, tokens), lambda at: (at, 0, 0))],
        out_specs=pl.BlockSpec((1, ROWS, SPAN), lambda at: (at, 0, 0)),
        compiler_params=params(8),
        cost_estimate=pl.CostEstimate(
            flops=4 * HEADS_HERE * tokens * tokens,
            bytes_accessed=4 * HEADS_HERE * tokens * tokens,
            transcendentals=0,
        ),
        name="offsets",
    )(*place(pltpu.HBM, grad_logits))

    back = lax.all_to_all(grads, "seq", split_axis=0, concat_axis=0, tiled=True)

    sums = jnp.sum(bias_part.reshape(HEADS_HERE, ROWS, SPAN // ROWS, ROWS), axis=(1, 3))
    sums = jnp.concatenate(
        [sums[:, :frame_count][:, ::-1], sums[:, frame_count + 1 :][:, ::-1]], axis=1
    ) / jnp.sqrt(WIDE(lax.axis_size("dp") * frame_count * patches))
    sums = lax.dynamic_update_slice_in_dim(
        jnp.zeros((THEADS, 2 * frame_count - 1), WIDE), sums, half * HEADS_HERE, 0
    )
    for axis, steps in (("dp", (1,)), ("dp", (2, 4, 6)), ("seq", (1, 2, 3))):
        sums = exchange_sum(sums, axis, steps)
    sums = split_sum(sums, (0, 4, 8, 12), (16, 20, 24, 28))
    back, sums = lax.optimization_barrier((back, sums))
    bias_grad = exchange_sum(sums, "dp", (1,))

    outputs = pl.pallas_call(
        unpack_kernel,
        out_shape=[pltpu.HBM((groups, ROWS, columns), LOW)] * 3,
        in_specs=[spec(pl.ANY)] * 4,
        out_specs=[spec(pl.ANY)] * 3,
        scratch_shapes=[pltpu.SemaphoreType.DMA((3 * HALVES,))],
        input_output_aliases={1: 0, 2: 1, 3: 2},
        compiler_params=params(8),
        cost_estimate=pl.CostEstimate(
            flops=0, bytes_accessed=12 * patches * SPATIAL, transcendentals=0
        ),
        name="unpack",
    )(
        back.reshape(groups, HALVES, 3, ROWS, WIDTH),
        *place(pltpu.HBM, *(tensor.reshape(groups, ROWS, columns) for tensor in spatial)),
    )
    shaped = tuple(tensor.reshape(1, 1, patches, columns) for tensor in outputs)
    return (*shaped, bias_grad)


def solution(mesh):
    split = P("dp", "seq", None, None)
    return jax.shard_map(
        local,
        mesh=mesh,
        in_specs=(split, split, split, split, P(), P()),
        out_specs=(split, split, split, P()),
        check_vma=False,
    )
```

```python
import functools

import jax
import jax.numpy as jnp
from jax import lax
from jax.experimental import pallas as pl
from jax.experimental.pallas import tpu as pltpu
from jax.sharding import PartitionSpec as P

SHEADS = 24
THEADS = 24
HDIM = 128
ROWS = 8
HALVES = 2
HEADS_HERE = THEADS // HALVES
WIDTH = HEADS_HERE * HDIM
SPATIAL = SHEADS * HDIM
SPAN = 512
NEG = -1e30
LOG2E = 1.4426950408889634
WIDE = jnp.float32
LOW = jnp.bfloat16
SCALE = HDIM ** (-0.5)
MIB = 1024 * 1024

NT = (((1,), (1,)), ((), ()))
NN = (((1,), (0,)), ((), ()))
TN = (((0,), (0,)), ((), ()))


def dot(left, right, dims):
    return lax.dot_general(left, right, dims, preferred_element_type=WIDE)


def products(query, keys, values, grad):
    return dot(keys, query, NT), dot(values, grad, NT)


def soften(logits, grad_attention, extra):
    logits = logits * (SCALE * LOG2E)
    if extra is not None:
        logits = logits + extra
    exponent = jnp.exp2(logits - jnp.max(logits, axis=0, keepdims=True))
    attention = exponent * (1.0 / jnp.sum(exponent, axis=0, keepdims=True))
    row_delta = jnp.sum(attention * grad_attention, axis=0, keepdims=True)
    return attention.astype(LOW), attention * (grad_attention - row_delta)


def token_grads(attention_low, grad_low, query, keys, grad):
    grad_query = (dot(grad_low, keys, TN) * SCALE).astype(LOW)
    grad_keys = (dot(grad_low, query, NN) * SCALE).astype(LOW)
    grad_values = dot(attention_low, grad, NN).astype(LOW)
    return grad_query, grad_keys, grad_values


def pack_kernel(query, keys, values, grad, packed, staged, in_sems, out_sems):
    reads, writes = [], []
    for number, source in enumerate((query, keys, values, grad)):
        for half in range(HALVES):
            at = number * HALVES + half
            reads.append(
                pltpu.make_async_copy(
                    source.at[:, :, pl.ds(SPATIAL + half * WIDTH, WIDTH)],
                    staged.at[:, half, number],
                    in_sems.at[at],
                )
            )
            writes.append(
                pltpu.make_async_copy(
                    staged.at[:, half, number], packed.at[:, half, number], out_sems.at[at]
                )
            )
    for copy in reads:
        copy.start()
    for read, write in zip(reads, writes):
        read.wait()
        write.start()
    for copy in writes:
        copy.wait()


def unpack_kernel(back, query_in, keys_in, values_in, query, keys, values, sems):
    copies = []
    for number, target in enumerate((query, keys, values)):
        for half in range(HALVES):
            copies.append(
                pltpu.make_async_copy(
                    back.at[:, half, number],
                    target.at[:, :, pl.ds(SPATIAL + half * WIDTH, WIDTH)],
                    sems.at[number * HALVES + half],
                )
            )
    for copy in copies:
        copy.start()
    for copy in copies:
        copy.wait()


def spatial_kernel(heads, live, query, keys, values, grad, grad_query, grad_keys, grad_values):
    flag = live[0].astype(WIDE).astype(LOW)
    for head in range(heads):
        cols = pl.ds(head * HDIM, HDIM)
        tokens = query[:, cols], keys[:, cols], values[:, cols], grad[:, cols] * flag
        attention_low, grad_logits = soften(*products(*tokens), None)
        outs = token_grads(
            attention_low, grad_logits.astype(LOW), tokens[0], tokens[1], tokens[3]
        )
        grad_query[:, cols] = outs[0]
        grad_keys[:, cols] = outs[1]
        grad_values[:, cols] = outs[2]


def moved_rows(seed, frame_count, length):
    blocks = SPAN // HDIM
    turns = HDIM // ROWS
    wide = frame_count * ROWS // HDIM
    rows = [None] * frame_count
    for turn in range(turns):
        moved = pltpu.roll(seed, turn * ROWS, 1) if turn else seed
        pieces = [moved[:, at * HDIM : (at + 1) * HDIM] for at in range(blocks)]
        for frame in range(turn, frame_count, turns):
            shift = frame // turns
            joined = jnp.concatenate([pieces[(at - shift) % blocks] for at in range(wide)], axis=1)
            rows[frame] = jnp.where(frame < length, joined, NEG)
    return jnp.concatenate(rows, axis=0)


def offset_sums(terms, frame_count):
    blocks = SPAN // HDIM
    turns = HDIM // ROWS
    wide = frame_count * ROWS // HDIM
    parts = []
    for turn in range(turns):
        pieces = [None] * blocks
        for frame in range(turn, frame_count, turns):
            for at in range(wide):
                to = (at - frame // turns) % blocks
                piece = terms[frame][:, at * HDIM : (at + 1) * HDIM]
                pieces[to] = piece if pieces[to] is None else pieces[to] + piece
        pieces = [jnp.zeros((ROWS, HDIM), WIDE) if piece is None else piece for piece in pieces]
        parts.append(jnp.concatenate(pieces, axis=1))
    step = ROWS
    while len(parts) > 1:
        parts = [
            parts[at] + pltpu.roll(parts[at + 1], SPAN - step, 1)
            for at in range(0, len(parts), 2)
        ]
        step *= 2
    return parts[0]


def temporal_kernel(frame_count, length, tensors, seed, grads, grad_logits, staged, kept, sems):
    tokens = frame_count * ROWS
    live_rows = lax.broadcasted_iota(jnp.int32, (tokens, HDIM), 0) < length[0] * ROWS
    copies = []

    def load(head):
        cols = pl.ds(head * HDIM, HDIM)
        query, keys, values, grad = (
            tensors[:, number, :, cols].reshape(tokens, HDIM) for number in range(4)
        )
        return query, keys, values, jnp.where(live_rows, grad.astype(WIDE), 0.0).astype(LOW)

    def send(source, target, at):
        copy = pltpu.make_async_copy(source, target, sems.at[at])
        copy.start()
        copies.append(copy)

    def finish(head, held, attention_low, grad_low):
        outs = token_grads(attention_low, grad_low, held[0], held[1], held[3])
        for number in range(3):
            staged[:, number, :, pl.ds(head * HDIM, HDIM)] = outs[number].reshape(
                frame_count, ROWS, HDIM
            )
        if head % 2:
            cols = pl.ds((head - 1) * HDIM, 2 * HDIM)
            send(staged.at[:, :, :, cols], grads.at[:, :, :, cols], HEADS_HERE + head // 2)

    held = load(0)
    ready = products(*held)
    waiting = None
    for head in range(HEADS_HERE):
        held_next = ready_next = None
        if head + 1 < HEADS_HERE:
            held_next = load(head + 1)
            ready_next = products(*held_next)
        table = moved_rows(seed[head], frame_count, length[0])
        attention_low, logits_grad = soften(*ready, table)
        kept[head] = logits_grad
        send(kept.at[head], grad_logits.at[head], head)
        if waiting is not None:
            finish(*waiting)
        waiting = head, held, attention_low, logits_grad.astype(LOW)
        held, ready = held_next, ready_next
    finish(*waiting)
    for copy in copies:
        copy.wait()


def bias_kernel(frame_count, terms, sums):
    sums[0] = offset_sums(terms[0].reshape(frame_count, ROWS, -1), frame_count)


def spec(space):
    return pl.BlockSpec(memory_space=space)


def place(space, *arrays):
    return [pltpu.with_memory_space_constraint(array, space) for array in arrays]


def params(limit):
    return pltpu.CompilerParams(vmem_limit_bytes=limit * MIB)


def tree_sum(pieces):
    while len(pieces) > 1:
        pieces = [pieces[at] + pieces[at + 1] for at in range(0, len(pieces), 2)]
    return pieces[0]


def exchange_sum(value, axis, steps):
    count = lax.axis_size(axis)
    return tree_sum(
        [value]
        + [lax.ppermute(value, axis, [(at, at ^ step) for at in range(count)]) for step in steps]
    )


def split_sum(value, low_steps, high_steps):
    clips, count = lax.axis_size("dp"), lax.axis_size("seq")
    pieces = []
    for steps in zip(low_steps, high_steps):
        pairs = [
            (clip * count + at, clip * count + (at ^ steps[clip % 2]))
            for clip in range(clips)
            for at in range(count)
        ]
        pieces.append(lax.ppermute(value, ("dp", "seq"), pairs))
    return tree_sum(pieces)


def local(query, keys, values, grad_out, frames, bias):
    frame_count = lax.axis_size("seq")
    frame_index = lax.axis_index("seq")
    length = lax.dynamic_index_in_dim(frames, lax.axis_index("dp"), 0, keepdims=True)
    live = (frame_index < length).astype(jnp.int32)
    patches, columns = query.shape[2], query.shape[3]
    groups = patches // ROWS
    tokens = frame_count * ROWS
    flat = [tensor.reshape(patches, columns) for tensor in (query, keys, values, grad_out)]
    tiled = [tensor.reshape(groups, ROWS, columns) for tensor in flat]

    packed = pl.pallas_call(
        pack_kernel,
        out_shape=pltpu.HBM((groups, HALVES, 4, ROWS, WIDTH), LOW),
        in_specs=[spec(pl.ANY)] * 4,
        out_specs=spec(pl.ANY),
        scratch_shapes=[
            pltpu.VMEM((groups, HALVES, 4, ROWS, WIDTH), LOW),
            pltpu.SemaphoreType.DMA((4 * HALVES,)),
            pltpu.SemaphoreType.DMA((4 * HALVES,)),
        ],
        compiler_params=params(8),
        name="pack",
    )(*place(pltpu.HBM, *tiled))
    gathered = lax.all_to_all(
        packed.reshape(frame_count, 4, ROWS, WIDTH), "seq", split_axis=0, concat_axis=0, tiled=True
    )

    heads = 4
    block = pl.BlockSpec((patches, heads * HDIM), lambda at, live: (0, at))
    spatial = pl.pallas_call(
        functools.partial(spatial_kernel, heads),
        out_shape=[pltpu.HBM((patches, columns), LOW)] * 3,
        grid_spec=pltpu.PrefetchScalarGridSpec(
            num_scalar_prefetch=1,
            grid=(SHEADS // heads,),
            in_specs=[block] * 4,
            out_specs=[block] * 3,
        ),
        compiler_params=params(16),
        cost_estimate=pl.CostEstimate(
            flops=10 * SHEADS * patches * patches * HDIM,
            bytes_accessed=14 * patches * SPATIAL,
            transcendentals=SHEADS * patches * patches,
        ),
        name="spatial",
    )(live, *place(pltpu.HBM, *flat))

    half = frame_index % HALVES
    bias_here = lax.dynamic_slice_in_dim(bias, half * HEADS_HERE, HEADS_HERE, 0)
    bias_here = bias_here * LOG2E
    offsets = jnp.concatenate(
        [
            bias_here[:, :frame_count][:, ::-1],
            jnp.full((HEADS_HERE, 1), NEG, WIDE),
            bias_here[:, frame_count:][:, ::-1],
        ],
        axis=1,
    )
    seed = jnp.where(
        jnp.eye(ROWS, dtype=bool)[None, :, None, :], offsets[:, None, :, None], NEG
    ).reshape(HEADS_HERE, ROWS, SPAN)
    gathered, *spatial = lax.optimization_barrier((gathered, *spatial))
    grads, grad_logits = pl.pallas_call(
        functools.partial(temporal_kernel, frame_count),
        out_shape=[
            pltpu.HBM((frame_count, 3, ROWS, WIDTH), LOW),
            pltpu.HBM((HEADS_HERE, tokens, tokens), WIDE),
        ],
        in_specs=[spec(pltpu.SMEM), spec(pltpu.VMEM), spec(pltpu.VMEM)],
        out_specs=[spec(pl.ANY)] * 2,
        scratch_shapes=[
            pltpu.VMEM((frame_count, 3, ROWS, WIDTH), LOW),
            pltpu.VMEM((HEADS_HERE, tokens, tokens), WIDE),
            pltpu.SemaphoreType.DMA((HEADS_HERE + HEADS_HERE // 2,)),
        ],
        compiler_params=params(24),
        cost_estimate=pl.CostEstimate(
            flops=10 * HEADS_HERE * tokens * tokens * HDIM,
            bytes_accessed=14 * tokens * WIDTH,
            transcendentals=HEADS_HERE * tokens * tokens,
        ),
        name="temporal",
    )(length, *place(pltpu.VMEM, gathered, seed))
    bias_part = pl.pallas_call(
        functools.partial(bias_kernel, frame_count),
        out_shape=jax.ShapeDtypeStruct((HEADS_HERE, ROWS, SPAN), WIDE),
        grid=(HEADS_HERE,),
        in_specs=[pl.BlockSpec((1, tokens, tokens), lambda at: (at, 0, 0))],
        out_specs=pl.BlockSpec((1, ROWS, SPAN), lambda at: (at, 0, 0)),
        compiler_params=params(8),
        cost_estimate=pl.CostEstimate(
            flops=4 * HEADS_HERE * tokens * tokens,
            bytes_accessed=4 * HEADS_HERE * tokens * tokens,
            transcendentals=0,
        ),
        name="offsets",
    )(*place(pltpu.HBM, grad_logits))

    back = lax.all_to_all(grads, "seq", split_axis=0, concat_axis=0, tiled=True)

    sums = jnp.sum(bias_part.reshape(HEADS_HERE, ROWS, SPAN // ROWS, ROWS), axis=(1, 3))
    sums = jnp.concatenate(
        [sums[:, :frame_count][:, ::-1], sums[:, frame_count + 1 :][:, ::-1]], axis=1
    ) / jnp.sqrt(WIDE(lax.axis_size("dp") * frame_count * patches))
    sums = lax.dynamic_update_slice_in_dim(
        jnp.zeros((THEADS, 2 * frame_count - 1), WIDE), sums, half * HEADS_HERE, 0
    )
    for axis, steps in (("dp", (1,)), ("dp", (2, 4, 6)), ("seq", (1, 2, 3))):
        sums = exchange_sum(sums, axis, steps)
    sums = split_sum(sums, (0, 4, 8, 12), (16, 20, 24, 28))
    other = lax.ppermute(
        sums, "dp", [(clip, clip ^ 1) for clip in range(lax.axis_size("dp"))]
    )

    outputs = pl.pallas_call(
        unpack_kernel,
        out_shape=[pltpu.HBM((groups, ROWS, columns), LOW)] * 3,
        in_specs=[spec(pl.ANY)] * 4,
        out_specs=[spec(pl.ANY)] * 3,
        scratch_shapes=[pltpu.SemaphoreType.DMA((3 * HALVES,))],
        input_output_aliases={1: 0, 2: 1, 3: 2},
        compiler_params=params(8),
        cost_estimate=pl.CostEstimate(
            flops=0, bytes_accessed=12 * patches * SPATIAL, transcendentals=0
        ),
        name="unpack",
    )(
        back.reshape(groups, HALVES, 3, ROWS, WIDTH),
        *place(pltpu.HBM, *(tensor.reshape(groups, ROWS, columns) for tensor in spatial)),
    )
    *outputs, other = lax.optimization_barrier((*outputs, other))
    bias_grad = sums + other
    shaped = tuple(tensor.reshape(1, 1, patches, columns) for tensor in outputs)
    return (*shaped, bias_grad)


def solution(mesh):
    split = P("dp", "seq", None, None)
    return jax.shard_map(
        local,
        mesh=mesh,
        in_specs=(split, split, split, split, P(), P()),
        out_specs=(split, split, split, P()),
        check_vma=False,
    )
```

```python
import functools

import jax
import jax.numpy as jnp
from jax import lax
from jax.experimental import pallas as pl
from jax.experimental.pallas import tpu as pltpu
from jax.sharding import PartitionSpec as P

SHEADS = 24
THEADS = 24
HDIM = 128
ROWS = 8
HALVES = 2
HEADS_HERE = THEADS // HALVES
WIDTH = HEADS_HERE * HDIM
SPATIAL = SHEADS * HDIM
SPAN = 512
NEG = -1e30
LOG2E = 1.4426950408889634
WIDE = jnp.float32
LOW = jnp.bfloat16
SCALE = HDIM ** (-0.5)
MIB = 1024 * 1024

NT = (((1,), (1,)), ((), ()))
NN = (((1,), (0,)), ((), ()))
TN = (((0,), (0,)), ((), ()))


def dot(left, right, dims):
    return lax.dot_general(left, right, dims, preferred_element_type=WIDE)


def products(query, keys, values, grad):
    return dot(keys, query, NT), dot(values, grad, NT)


def soften(logits, grad_attention, extra):
    logits = logits * (SCALE * LOG2E)
    if extra is not None:
        logits = logits + extra
    exponent = jnp.exp2(logits - jnp.max(logits, axis=0, keepdims=True))
    attention = exponent * (1.0 / jnp.sum(exponent, axis=0, keepdims=True))
    row_delta = jnp.sum(attention * grad_attention, axis=0, keepdims=True)
    return attention.astype(LOW), attention * (grad_attention - row_delta)


def token_grads(attention_low, grad_low, query, keys, grad):
    grad_query = (dot(grad_low, keys, TN) * SCALE).astype(LOW)
    grad_keys = (dot(grad_low, query, NN) * SCALE).astype(LOW)
    grad_values = dot(attention_low, grad, NN).astype(LOW)
    return grad_query, grad_keys, grad_values


def pack_kernel(query, keys, values, grad, packed, staged, in_sems, out_sems):
    reads, writes = [], []
    for number, source in enumerate((query, keys, values, grad)):
        for half in range(HALVES):
            at = number * HALVES + half
            reads.append(
                pltpu.make_async_copy(
                    source.at[:, :, pl.ds(SPATIAL + half * WIDTH, WIDTH)],
                    staged.at[:, half, number],
                    in_sems.at[at],
                )
            )
            writes.append(
                pltpu.make_async_copy(
                    staged.at[:, half, number], packed.at[:, half, number], out_sems.at[at]
                )
            )
    for copy in reads:
        copy.start()
    for read, write in zip(reads, writes):
        read.wait()
        write.start()
    for copy in writes:
        copy.wait()


def unpack_kernel(back, query_in, keys_in, values_in, query, keys, values, sems):
    copies = []
    for number, target in enumerate((query, keys, values)):
        for half in range(HALVES):
            copies.append(
                pltpu.make_async_copy(
                    back.at[:, half, number],
                    target.at[:, :, pl.ds(SPATIAL + half * WIDTH, WIDTH)],
                    sems.at[number * HALVES + half],
                )
            )
    for copy in copies:
        copy.start()
    for copy in copies:
        copy.wait()


def spatial_kernel(heads, core, frames, place_here, query, keys, values, grad, *outputs):
    grad_query, grad_keys, grad_values = outputs[-3:]

    @pl.when(place_here[0] % 2 == core)
    def _():
        flag = jnp.where(place_here[1] < frames[place_here[0]], 1.0, 0.0).astype(LOW)
        for head in range(heads):
            cols = pl.ds(head * HDIM, HDIM)
            tokens = query[:, cols], keys[:, cols], values[:, cols], grad[:, cols] * flag
            attention_low, grad_logits = soften(*products(*tokens), None)
            outs = token_grads(
                attention_low, grad_logits.astype(LOW), tokens[0], tokens[1], tokens[3]
            )
            grad_query[:, cols] = outs[0]
            grad_keys[:, cols] = outs[1]
            grad_values[:, cols] = outs[2]


def moved_rows(seed, frame_count, length):
    blocks = SPAN // HDIM
    turns = HDIM // ROWS
    wide = frame_count * ROWS // HDIM
    rows = [None] * frame_count
    for turn in range(turns):
        moved = pltpu.roll(seed, turn * ROWS, 1) if turn else seed
        pieces = [moved[:, at * HDIM : (at + 1) * HDIM] for at in range(blocks)]
        for frame in range(turn, frame_count, turns):
            shift = frame // turns
            joined = jnp.concatenate([pieces[(at - shift) % blocks] for at in range(wide)], axis=1)
            rows[frame] = jnp.where(frame < length, joined, NEG)
    return jnp.concatenate(rows, axis=0)


def offset_sums(terms, frame_count):
    blocks = SPAN // HDIM
    turns = HDIM // ROWS
    wide = frame_count * ROWS // HDIM
    parts = []
    for turn in range(turns):
        pieces = [None] * blocks
        for frame in range(turn, frame_count, turns):
            for at in range(wide):
                to = (at - frame // turns) % blocks
                piece = terms[frame][:, at * HDIM : (at + 1) * HDIM]
                pieces[to] = piece if pieces[to] is None else pieces[to] + piece
        pieces = [jnp.zeros((ROWS, HDIM), WIDE) if piece is None else piece for piece in pieces]
        parts.append(jnp.concatenate(pieces, axis=1))
    step = ROWS
    while len(parts) > 1:
        parts = [
            parts[at] + pltpu.roll(parts[at + 1], SPAN - step, 1)
            for at in range(0, len(parts), 2)
        ]
        step *= 2
    return parts[0]


def temporal_kernel(frame_count, length, tensors, seed, grads, grad_logits, staged, kept, sems):
    tokens = frame_count * ROWS
    live_rows = lax.broadcasted_iota(jnp.int32, (tokens, HDIM), 0) < length[0] * ROWS
    copies = []

    def load(head):
        cols = pl.ds(head * HDIM, HDIM)
        query, keys, values, grad = (
            tensors[:, number, :, cols].reshape(tokens, HDIM) for number in range(4)
        )
        return query, keys, values, jnp.where(live_rows, grad.astype(WIDE), 0.0).astype(LOW)

    def send(source, target, at):
        copy = pltpu.make_async_copy(source, target, sems.at[at])
        copy.start()
        copies.append(copy)

    def finish(head, held, attention_low, grad_low):
        outs = token_grads(attention_low, grad_low, held[0], held[1], held[3])
        for number in range(3):
            staged[:, number, :, pl.ds(head * HDIM, HDIM)] = outs[number].reshape(
                frame_count, ROWS, HDIM
            )
        if head % 2:
            cols = pl.ds((head - 1) * HDIM, 2 * HDIM)
            send(staged.at[:, :, :, cols], grads.at[:, :, :, cols], HEADS_HERE + head // 2)

    held = load(0)
    ready = products(*held)
    waiting = None
    for head in range(HEADS_HERE):
        held_next = ready_next = None
        if head + 1 < HEADS_HERE:
            held_next = load(head + 1)
            ready_next = products(*held_next)
        table = moved_rows(seed[head], frame_count, length[0])
        attention_low, logits_grad = soften(*ready, table)
        kept[head] = logits_grad
        send(kept.at[head], grad_logits.at[head], head)
        if waiting is not None:
            finish(*waiting)
        waiting = head, held, attention_low, logits_grad.astype(LOW)
        held, ready = held_next, ready_next
    finish(*waiting)
    for copy in copies:
        copy.wait()


def bias_kernel(frame_count, terms, sums):
    sums[0] = offset_sums(terms[0].reshape(frame_count, ROWS, -1), frame_count)


def spec(space):
    return pl.BlockSpec(memory_space=space)


def place(space, *arrays):
    return [pltpu.with_memory_space_constraint(array, space) for array in arrays]


def params(limit):
    return pltpu.CompilerParams(vmem_limit_bytes=limit * MIB)


def tree_sum(pieces):
    while len(pieces) > 1:
        pieces = [pieces[at] + pieces[at + 1] for at in range(0, len(pieces), 2)]
    return pieces[0]


def exchange_sum(value, axis, steps):
    count = lax.axis_size(axis)
    return tree_sum(
        [value]
        + [lax.ppermute(value, axis, [(at, at ^ step) for at in range(count)]) for step in steps]
    )


def split_sum(value, low_steps, high_steps):
    clips, count = lax.axis_size("dp"), lax.axis_size("seq")
    pieces = []
    for steps in zip(low_steps, high_steps):
        pairs = [
            (clip * count + at, clip * count + (at ^ steps[clip % 2]))
            for clip in range(clips)
            for at in range(count)
        ]
        pieces.append(lax.ppermute(value, ("dp", "seq"), pairs))
    return tree_sum(pieces)


def local(query, keys, values, grad_out, frames, bias):
    frame_count = lax.axis_size("seq")
    frame_index = lax.axis_index("seq")
    length = lax.dynamic_index_in_dim(frames, lax.axis_index("dp"), 0, keepdims=True)
    patches, columns = query.shape[2], query.shape[3]
    groups = patches // ROWS
    tokens = frame_count * ROWS
    flat = [tensor.reshape(patches, columns) for tensor in (query, keys, values, grad_out)]
    tiled = [tensor.reshape(groups, ROWS, columns) for tensor in flat]

    packed = pl.pallas_call(
        pack_kernel,
        out_shape=pltpu.HBM((groups, HALVES, 4, ROWS, WIDTH), LOW),
        in_specs=[spec(pl.ANY)] * 4,
        out_specs=spec(pl.ANY),
        scratch_shapes=[
            pltpu.VMEM((groups, HALVES, 4, ROWS, WIDTH), LOW),
            pltpu.SemaphoreType.DMA((4 * HALVES,)),
            pltpu.SemaphoreType.DMA((4 * HALVES,)),
        ],
        compiler_params=params(8),
        name="pack",
    )(*place(pltpu.HBM, *tiled))
    heads = 4
    blocks = SHEADS // heads
    place_here = jnp.stack([lax.axis_index("dp"), frame_index]).astype(jnp.int32)

    def spatial_part(core, earlier):
        block = pl.BlockSpec(
            (patches, heads * HDIM),
            lambda at, frames, here: (0, jnp.where(here[0] % 2 == core, at, blocks)),
        )
        return pl.pallas_call(
            functools.partial(spatial_kernel, heads, core),
            out_shape=[pltpu.HBM((patches, columns), LOW)] * 3,
            grid_spec=pltpu.PrefetchScalarGridSpec(
                num_scalar_prefetch=2,
                grid=(blocks,),
                in_specs=[block] * 4 + [spec(pl.ANY)] * len(earlier),
                out_specs=[block] * 3,
            ),
            input_output_aliases={6 + number: number for number in range(len(earlier))},
            compiler_params=params(16),
            cost_estimate=pl.CostEstimate(
                flops=10 * SHEADS * patches * patches * HDIM,
                bytes_accessed=14 * patches * SPATIAL,
                transcendentals=SHEADS * patches * patches,
            ),
            name="spatial",
        )(
            frames,
            place_here,
            *place(pltpu.HBM, *flat, *earlier),
        )

    spatial = spatial_part(0, ())
    packed, *spatial = lax.optimization_barrier((packed, *spatial))
    gathered = lax.all_to_all(
        packed.reshape(frame_count, 4, ROWS, WIDTH), "seq", split_axis=0, concat_axis=0, tiled=True
    )
    spatial = spatial_part(1, spatial)

    half = frame_index % HALVES
    bias_here = lax.dynamic_slice_in_dim(bias, half * HEADS_HERE, HEADS_HERE, 0)
    bias_here = bias_here * LOG2E
    offsets = jnp.concatenate(
        [
            bias_here[:, :frame_count][:, ::-1],
            jnp.full((HEADS_HERE, 1), NEG, WIDE),
            bias_here[:, frame_count:][:, ::-1],
        ],
        axis=1,
    )
    seed = jnp.where(
        jnp.eye(ROWS, dtype=bool)[None, :, None, :], offsets[:, None, :, None], NEG
    ).reshape(HEADS_HERE, ROWS, SPAN)
    gathered, *spatial = lax.optimization_barrier((gathered, *spatial))
    grads, grad_logits = pl.pallas_call(
        functools.partial(temporal_kernel, frame_count),
        out_shape=[
            pltpu.HBM((frame_count, 3, ROWS, WIDTH), LOW),
            pltpu.HBM((HEADS_HERE, tokens, tokens), WIDE),
        ],
        in_specs=[spec(pltpu.SMEM), spec(pltpu.VMEM), spec(pltpu.VMEM)],
        out_specs=[spec(pl.ANY)] * 2,
        scratch_shapes=[
            pltpu.VMEM((frame_count, 3, ROWS, WIDTH), LOW),
            pltpu.VMEM((HEADS_HERE, tokens, tokens), WIDE),
            pltpu.SemaphoreType.DMA((HEADS_HERE + HEADS_HERE // 2,)),
        ],
        compiler_params=params(24),
        cost_estimate=pl.CostEstimate(
            flops=10 * HEADS_HERE * tokens * tokens * HDIM,
            bytes_accessed=14 * tokens * WIDTH,
            transcendentals=HEADS_HERE * tokens * tokens,
        ),
        name="temporal",
    )(length, *place(pltpu.VMEM, gathered, seed))
    bias_part = pl.pallas_call(
        functools.partial(bias_kernel, frame_count),
        out_shape=jax.ShapeDtypeStruct((HEADS_HERE, ROWS, SPAN), WIDE),
        grid=(HEADS_HERE,),
        in_specs=[pl.BlockSpec((1, tokens, tokens), lambda at: (at, 0, 0))],
        out_specs=pl.BlockSpec((1, ROWS, SPAN), lambda at: (at, 0, 0)),
        compiler_params=params(8),
        cost_estimate=pl.CostEstimate(
            flops=4 * HEADS_HERE * tokens * tokens,
            bytes_accessed=4 * HEADS_HERE * tokens * tokens,
            transcendentals=0,
        ),
        name="offsets",
    )(*place(pltpu.HBM, grad_logits))

    back = lax.all_to_all(grads, "seq", split_axis=0, concat_axis=0, tiled=True)

    sums = jnp.sum(bias_part.reshape(HEADS_HERE, ROWS, SPAN // ROWS, ROWS), axis=(1, 3))
    sums = jnp.concatenate(
        [sums[:, :frame_count][:, ::-1], sums[:, frame_count + 1 :][:, ::-1]], axis=1
    ) / jnp.sqrt(WIDE(lax.axis_size("dp") * frame_count * patches))
    sums = lax.dynamic_update_slice_in_dim(
        jnp.zeros((THEADS, 2 * frame_count - 1), WIDE), sums, half * HEADS_HERE, 0
    )
    for axis, steps in (("dp", (1,)), ("dp", (2, 4, 6)), ("seq", (1, 2, 3))):
        sums = exchange_sum(sums, axis, steps)
    sums = split_sum(sums, (0, 4, 8, 12), (16, 20, 24, 28))
    other = lax.ppermute(
        sums, "dp", [(clip, clip ^ 1) for clip in range(lax.axis_size("dp"))]
    )

    outputs = pl.pallas_call(
        unpack_kernel,
        out_shape=[pltpu.HBM((groups, ROWS, columns), LOW)] * 3,
        in_specs=[spec(pl.ANY)] * 4,
        out_specs=[spec(pl.ANY)] * 3,
        scratch_shapes=[pltpu.SemaphoreType.DMA((3 * HALVES,))],
        input_output_aliases={1: 0, 2: 1, 3: 2},
        compiler_params=params(8),
        cost_estimate=pl.CostEstimate(
            flops=0, bytes_accessed=12 * patches * SPATIAL, transcendentals=0
        ),
        name="unpack",
    )(
        back.reshape(groups, HALVES, 3, ROWS, WIDTH),
        *place(pltpu.HBM, *(tensor.reshape(groups, ROWS, columns) for tensor in spatial)),
    )
    *outputs, other = lax.optimization_barrier((*outputs, other))
    bias_grad = sums + other
    shaped = tuple(tensor.reshape(1, 1, patches, columns) for tensor in outputs)
    return (*shaped, bias_grad)


def solution(mesh):
    split = P("dp", "seq", None, None)
    return jax.shard_map(
        local,
        mesh=mesh,
        in_specs=(split, split, split, split, P(), P()),
        out_specs=(split, split, split, P()),
        check_vma=False,
    )
```
